32 devices in a mesh: gx: 4 (over y, x), gy: 4 (over z), gz: 2 (over core).
Axes of the slice: x: 2, y: 2, z: 4, core: 2. Of those that a mesh axis runs over, the one named last changes fastest.
Arguments:
- offsets: float32 [3, 16, 16, 8, 128], P(None, 'gx', 'gy', 'gz'), may hold values from 0 to 1
- masses: float32 [16, 16, 8, 128], P('gx', 'gy', 'gz'), may hold values from 2e-05 to 0.0002
- counts: int32 [16, 16, 8], P('gx', 'gy', 'gz'), may hold values from 1 to 128, as said below
Outputs:
- potential: float32 [16, 16, 8, 128], P('gx', 'gy', 'gz')
- near_part: float32 [16, 16, 8, 128], P('gx', 'gy', 'gz')
- far_leaf: float32 [16, 16, 8, 128], P('gx', 'gy', 'gz')
The draws below stay inside these ranges and needn't reach their ends.
Inputs may be any that keep to these rules, and one draw needn't show every extreme that they name: counts gives the live slots of each leaf; slots from counts on have masses that do not enter; some leaf holds 128 particles.
All inputs are finite; a program needn't handle non-finite values.
Results may differ from the reference program's by a relative error of at most 0.0003.
Values sent between devices are 32-bit elements; how exact they have to be, the bound alone decides.
A program may use at most 320 MiB of HBM per device.

```python
import math
import jax
import jax.numpy as jnp
from jax import lax

SLOTS = 128
ORDER = 8
NX = 16
NY = 16
NZ = 8


def draw_offsets(key, part):
    key = jax.random.fold_in(key, 5)
    corner_key, spread_key = jax.random.split(key)
    corner = jax.random.randint(corner_key, (3, NX, NY, NZ, 1), 0, 2).astype(jnp.float32)
    spread = jax.random.uniform(spread_key, (3, NX, NY, NZ, SLOTS), jnp.float32)
    depth = 0.5 * spread * spread
    return corner * (1.0 - depth) + (1.0 - corner) * depth


def draw_counts(key, part):
    key = jax.random.fold_in(key, 11)
    raw_key, thin_key, full_key = jax.random.split(key, 3)
    raw_counts = jax.random.randint(raw_key, (NX, NY, NZ), 1, SLOTS + 1)
    shrink = jax.random.randint(thin_key, (NX // 4, NY // 4, NZ // 4), 0, 3)
    shrink = jnp.repeat(jnp.repeat(jnp.repeat(shrink, 4, 0), 4, 1), 4, 2)
    thinned = jnp.maximum(jnp.right_shift(raw_counts, shrink), 1)
    full_leaf = jax.random.randint(full_key, (), 0, NX * NY * NZ)
    return thinned.reshape(-1).at[full_leaf].set(SLOTS).reshape(NX, NY, NZ).astype(jnp.int32)


def level_of(stream_key, extent, cuts, smallest, largest):
    gain, own = 1.0, jax.random.fold_in(stream_key, 6)
    for dim, parts in cuts:
        steps = jnp.exp(jax.random.uniform(jax.random.fold_in(own, dim), (parts,), jnp.float32, smallest / len(cuts), largest / len(cuts)))
        gain = gain * jnp.repeat(steps, extent[dim] // parts).reshape([-1 if axis == dim else 1 for axis in range(len(extent))])
    return gain


def setup_inputs(seed: int = 0) -> dict:
    keys = jax.random.split(jax.random.key(seed), 4)
    return {
        "offsets": draw_offsets(jax.random.fold_in(keys[3], 71), 0),
        "masses": jnp.clip(jnp.exp(math.log(0.0002) - 2.3025851 * jax.random.uniform(keys[1], (NX, NY, NZ, SLOTS), jnp.float32) ** level_of(keys[1], (NX, NY, NZ, SLOTS), ((0, 4), (1, 4), (2, 2)), -0.2, 0.2)), 1.9999999494757503e-05, 0.0002),
        "counts": draw_counts(jax.random.fold_in(keys[3], 71), 0),
    }


HIGHEST = lax.Precision.HIGHEST
SOFTENING = 0.02

def expansion_tables(top_order):
    powers_list = []
    for degree in range(top_order + 1):
        for first_part in range(degree, -1, -1):
            for second_part in range(degree - first_part, -1, -1):
                powers_list.append((first_part, second_part, degree - first_part - second_part))
    position = {entry: number for number, entry in enumerate(powers_list)}
    return (powers_list, position)

def translation_tables(top_order):
    powers_list, position = expansion_tables(top_order)
    n_terms = len(powers_list)
    source_index = [[0] * n_terms for unused in range(n_terms)]
    weights = [[0.0] * n_terms for unused in range(n_terms)]
    for j_entry, j_power in enumerate(powers_list):
        for k_entry, k_power in enumerate(powers_list):
            joined = tuple((j_power[d] + k_power[d] for d in range(3)))
            if sum(joined) <= top_order:
                source_index[j_entry][k_entry] = position[joined]
                factor = (-1.0) ** sum(k_power)
                for d in range(3):
                    factor = factor * math.comb(joined[d], j_power[d])
                weights[j_entry][k_entry] = factor
    return (jnp.asarray(source_index, jnp.int32), jnp.asarray(weights, jnp.float32))

def shift_matrices(top_order, child_size):
    powers_list, position = expansion_tables(top_order)
    n_terms = len(powers_list)
    result = [[[0.0] * n_terms for unused in range(n_terms)] for other in range(8)]
    for child in range(8):
        bits = (child >> 2 & 1, child >> 1 & 1, child & 1)
        offset = [(bits[d] - 0.5) * child_size for d in range(3)]
        for k_entry, k_power in enumerate(powers_list):
            for i_entry, i_power in enumerate(powers_list):
                if all((i_power[d] <= k_power[d] for d in range(3))):
                    factor = 1.0
                    for d in range(3):
                        factor = factor * math.comb(k_power[d], i_power[d]) * offset[d] ** (k_power[d] - i_power[d])
                    result[child][k_entry][i_entry] = factor
    return jnp.asarray(result, jnp.float32)

def taylor_terms(vector, top_order):
    powers_list, position = expansion_tables(top_order)
    radius_sq = vector[0] * vector[0] + vector[1] * vector[1] + vector[2] * vector[2]
    taylor_rows = [1.0 / jnp.sqrt(radius_sq)]
    for entry in range(1, len(powers_list)):
        exponent = powers_list[entry]
        degree = sum(exponent)
        linear_part = jnp.zeros_like(radius_sq)
        square_part = jnp.zeros_like(radius_sq)
        for axis_id in range(3):
            if exponent[axis_id] >= 1:
                lowered = list(exponent)
                lowered[axis_id] -= 1
                linear_part = linear_part + vector[axis_id] * taylor_rows[position[tuple(lowered)]]
            if exponent[axis_id] >= 2:
                lowered = list(exponent)
                lowered[axis_id] -= 2
                square_part = square_part + taylor_rows[position[tuple(lowered)]]
        taylor_rows.append(-((2 * degree - 1) * linear_part + (degree - 1) * square_part) / (degree * radius_sq))
    return jnp.stack(taylor_rows)

def monomials(positions, top_order):
    powers_list, position = expansion_tables(top_order)
    centred = positions - 0.5
    picked = []
    for d in range(3):
        ladder = [jnp.ones_like(centred[d])]
        for step in range(top_order):
            ladder.append(ladder[-1] * centred[d])
        select = [[1.0 if entry[d] == level else 0.0 for level in range(top_order + 1)] for entry in powers_list]
        picked.append(jnp.tensordot(jnp.asarray(select, jnp.float32), jnp.stack(ladder), axes=1, precision=HIGHEST))
    return picked[0] * picked[1] * picked[2]

def near_field(window):
    a, b, c = (window.shape[1] - 2, window.shape[2] - 2, window.shape[3] - 2)
    centre = window[:, 1:-1, 1:-1, 1:-1]
    total = jnp.zeros(centre.shape[1:], jnp.float32)
    for p in range(3):
        for q in range(3):
            for r in range(3):
                source = window[:, p:p + a, q:q + b, r:r + c]
                squared = SOFTENING * SOFTENING
                for axis_id, shift in enumerate((p - 1, q - 1, r - 1)):
                    gap = source[axis_id][..., None, :] + float(shift) - centre[axis_id][..., :, None]
                    squared = squared + gap * gap
                total = total + lax.optimization_barrier(jnp.sum(source[3][..., None, :] / jnp.sqrt(squared), axis=-1))
    return total - centre[3] / SOFTENING

def window_kernel(step, top_order):
    source_index, weights = translation_tables(top_order)
    grid = jnp.arange(7, dtype=jnp.float32) - 3.0
    mesh = jnp.meshgrid(grid, grid, grid, indexing='ij')
    vx, vy, vz = [m.reshape(-1) for m in mesh]
    near = (jnp.abs(vx) <= 1.0) & (jnp.abs(vy) <= 1.0) & (jnp.abs(vz) <= 1.0)
    vector = jnp.stack([jnp.where(near, 4.0, -vx) * step, jnp.where(near, 0.0, -vy) * step, jnp.where(near, 0.0, -vz) * step])
    terms = taylor_terms(vector, top_order)
    kernel = terms[source_index] * weights[:, :, None]
    return jnp.transpose(kernel, (2, 0, 1))

def interaction_mask(extents, anchor):
    offsets_list = jnp.arange(7, dtype=jnp.int32) - 3
    valid = []
    for d in range(3):
        cells = jnp.arange(extents[d], dtype=jnp.int32) + anchor[d]
        moved = jnp.floor_divide(cells[None, :] + offsets_list[:, None], 2) - jnp.floor_divide(cells, 2)[None, :]
        valid.append(jnp.abs(moved) <= 1)
    far = jnp.abs(offsets_list) >= 2
    separated = far[:, None, None] | far[None, :, None] | far[None, None, :]
    mask = valid[0][:, None, None, :, None, None] & valid[1][None, :, None, None, :, None] & valid[2][None, None, :, None, None, :]
    mask = mask & separated[:, :, :, None, None, None]
    return mask.reshape(343, extents[0] * extents[1] * extents[2]).astype(jnp.float32)

def window_interactions(window, kernel, anchor):
    a, b, c, n_terms = (window.shape[0] - 6, window.shape[1] - 6, window.shape[2] - 6, window.shape[3])
    along_x = jnp.stack([window[s:s + a] for s in range(7)])
    along_y = jnp.stack([along_x[:, :, s:s + b] for s in range(7)], axis=1)
    along_z = jnp.stack([along_y[:, :, :, :, s:s + c] for s in range(7)], axis=2)
    gathered = along_z.reshape(343, a * b * c, n_terms) * interaction_mask((a, b, c), anchor)[:, :, None]
    result = jnp.einsum('vcm,vjm->cj', gathered, kernel, precision=HIGHEST)
    return result.reshape(a, b, c, n_terms)

def cell_centers(starts, extents, size):
    grids = jnp.meshgrid(*[jnp.arange(extents[d], dtype=jnp.int32) + starts[d] for d in range(3)], indexing='ij')
    return jnp.stack([g.reshape(-1).astype(jnp.float32) * size + 0.5 * size for g in grids], axis=1)

def pair_interactions(target_centers, source_moments, source_centers, step, top_order):
    source_index, weight_table = translation_tables(top_order)

    def one_target(center):

        def add_block(total, pieces):
            moments, centers = pieces
            gap = center[None, :] - centers
            near = lax.optimization_barrier(jnp.max(jnp.abs(gap), axis=1)) <= 1.5 * step
            vector = jnp.stack([jnp.where(near, 4.0 * step, gap[:, 0]), jnp.where(near, 0.0, gap[:, 1]), jnp.where(near, 0.0, gap[:, 2])])
            terms = taylor_terms(vector, top_order)
            kernel = terms[source_index] * weight_table[:, :, None]
            kept = moments * jnp.where(near, 0.0, 1.0)[:, None]
            return (total + jnp.einsum('jkb,bk->j', kernel, kept, precision=HIGHEST), None)
        start = jnp.zeros((source_moments.shape[-1],), jnp.float32)
        total, unused = lax.scan(add_block, start, (source_moments, source_centers))
        return total
    return lax.map(one_target, target_centers)

def up_shift(moments, matrices):
    a, b, c, n_terms = moments.shape
    grouped = moments.reshape(a // 2, 2, b // 2, 2, c // 2, 2, n_terms).transpose(0, 2, 4, 1, 3, 5, 6)
    grouped = grouped.reshape(a // 2, b // 2, c // 2, 8, n_terms)
    return jnp.einsum('xyzgi,gki->xyzk', grouped, matrices, precision=HIGHEST)

def down_shift(local, matrices):
    a, b, c, n_terms = local.shape
    spread = jnp.einsum('xyzk,gki->xyzgi', local, matrices, precision=HIGHEST)
    spread = spread.reshape(a, b, c, 2, 2, 2, n_terms).transpose(0, 3, 1, 4, 2, 5, 6)
    return spread.reshape(2 * a, 2 * b, 2 * c, n_terms)

def reference(offsets, masses, counts):
    extent_x, extent_y, extent_z = counts.shape
    slots = masses.shape[-1]
    live = (jnp.arange(slots, dtype=jnp.int32)[None, None, None, :] < counts[..., None]).astype(jnp.float32)
    charge = masses * live
    packed = jnp.concatenate([offsets, charge[None]], axis=0)
    padded = jnp.pad(packed, ((0, 0), (1, 1), (1, 1), (1, 1), (0, 0)))
    planes = jnp.arange(extent_x, dtype=jnp.int32)
    near = lax.map(lambda plane_index: near_field(lax.dynamic_slice_in_dim(padded, plane_index, 3, 1))[0], planes)

    def slab_rows(plane_index):
        positions = lax.dynamic_slice_in_dim(offsets, plane_index, 1, 1).reshape(3, extent_y * extent_z, slots)
        return monomials(positions, ORDER)

    def slab_moments(plane_index):
        weight = lax.dynamic_slice_in_dim(charge, plane_index, 1, 0).reshape(extent_y * extent_z, slots)
        moments = jnp.einsum('kts,ts->tk', slab_rows(plane_index), weight, precision=HIGHEST)
        return moments.reshape(extent_y, extent_z, -1)
    moments0 = lax.map(slab_moments, planes)
    n_terms = moments0.shape[-1]
    shift_leaf = shift_matrices(ORDER, 1.0)
    shift_mid = shift_matrices(ORDER, 2.0)
    moments1 = up_shift(moments0, shift_leaf)
    moments2 = up_shift(moments1, shift_mid)
    padded0 = jnp.pad(moments0, ((3, 3), (3, 3), (3, 3), (0, 0)))
    kernel0 = window_kernel(1.0, ORDER)
    local0 = lax.map(lambda plane_index: window_interactions(lax.dynamic_slice_in_dim(padded0, plane_index, 7, 0), kernel0, (plane_index, 0, 0))[0], planes)
    padded1 = jnp.pad(moments1, ((3, 3), (3, 3), (3, 3), (0, 0)))
    kernel1 = window_kernel(2.0, ORDER)
    mid_planes = jnp.arange(extent_x // 2, dtype=jnp.int32)
    local1 = lax.map(lambda plane_index: window_interactions(lax.dynamic_slice_in_dim(padded1, plane_index, 7, 0), kernel1, (plane_index, 0, 0))[0], mid_planes)
    top_shape = moments2.shape[:3]
    centers = cell_centers((0, 0, 0), top_shape, 4.0)
    sources = moments2.reshape(-1, top_shape[2], n_terms)
    source_centers = centers.reshape(-1, top_shape[2], 3)
    local2 = pair_interactions(centers, sources, source_centers, 4.0, ORDER).reshape(top_shape + (n_terms,))
    total1 = local1 + down_shift(local2, shift_mid)
    total0 = local0 + down_shift(total1, shift_leaf)

    def slab_far(plane_index):
        rows = slab_rows(plane_index)
        expansion = lax.dynamic_slice_in_dim(total0, plane_index, 1, 0).reshape(extent_y * extent_z, n_terms)
        leaf_only = lax.dynamic_slice_in_dim(local0, plane_index, 1, 0).reshape(extent_y * extent_z, n_terms)
        values = jnp.einsum('kts,tk->ts', rows, expansion, precision=HIGHEST)
        leaf_values = jnp.einsum('kts,tk->ts', rows, leaf_only, precision=HIGHEST)
        return (values.reshape(extent_y, extent_z, slots), leaf_values.reshape(extent_y, extent_z, slots))
    far, far_local = lax.map(slab_far, planes)
    return (-(near + far) * live, -near * live, -far_local * live)
```

```python
import functools
import math

import jax
import jax.numpy as jnp
import ml_dtypes
import numpy as np
from jax import lax
from jax.experimental import pallas as pl
from jax.experimental.pallas import tpu as pltpu
from jax.sharding import PartitionSpec as P

ORDER = 8
SOFTENING = 0.02
HIGHEST = lax.Precision.HIGHEST
LANES = 128
ROWS = 16
VMEM_BYTES = 48 * 1024 * 1024


def multi_indices():
    listed = []
    for degree in range(ORDER + 1):
        for first in range(degree, -1, -1):
            for second in range(degree - first, -1, -1):
                listed.append((first, second, degree - first - second))
    return listed


FULL = multi_indices()
BASIS = [n for n in FULL if n[2] <= 1]
SLOT = {n: i for i, n in enumerate(BASIS)}
TERMS = len(BASIS)


def fold_row(n):
    w = n[2] // 2
    return [
        (SLOT[(n[0] + 2 * u, n[1] + 2 * (w - u), n[2] - 2 * w)], (-1.0) ** w * math.comb(w, u))
        for u in range(w + 1)
    ]


def derivatives(vectors):
    r = [vectors[:, i] for i in range(3)]
    sq = r[0] ** 2 + r[1] ** 2 + r[2] ** 2
    a = {(0, 0, 0): 1.0 / np.sqrt(sq)}
    for n in FULL[1:]:
        d = sum(n)
        lin = np.zeros_like(sq)
        two = np.zeros_like(sq)
        for i in range(3):
            low = list(n)
            low[i] -= 1
            if low[i] >= 0:
                lin = lin + r[i] * a[tuple(low)]
            low[i] -= 1
            if low[i] >= 0:
                two = two + a[tuple(low)]
        a[n] = -((2 * d - 1) * lin + (d - 1) * two) / (d * sq)
    return {n: a[n] * math.prod(math.factorial(c) for c in n) for n in FULL}


def translation(offsets):
    offsets = np.asarray(offsets, np.float64)
    near = np.max(np.abs(offsets), axis=1) <= 1.5
    b = derivatives(np.where(near[:, None], [4.0, 0.0, 0.0], -offsets))
    out = np.zeros((len(offsets), LANES, LANES))
    for h, hn in enumerate(BASIS):
        for j, jn in enumerate(BASIS):
            n = tuple(hn[i] + jn[i] for i in range(3))
            if sum(n) <= ORDER:
                out[:, h, j] = np.where(near, 0.0, b[n])
    return out


def power_ratio(u, k):
    if min(k) < 0:
        return 0.0
    return math.prod(u[i] ** k[i] / math.factorial(k[i]) for i in range(3))


@functools.lru_cache(None)
def shift_tables():
    up = np.zeros((8, LANES, LANES))
    down = np.zeros((8, LANES, LANES))
    for g in range(8):
        u = [(g >> 2 & 1) - 0.5, (g >> 1 & 1) - 0.5, (g & 1) - 0.5]
        for n in FULL:
            scale = 0.5 ** sum(n)
            for h, coefficient in fold_row(n):
                for i, k in enumerate(BASIS):
                    gap = tuple(n[d] - k[d] for d in range(3))
                    up[g, i, h] += scale * coefficient * power_ratio([-c for c in u], gap)
                    down[g, h, i] += scale * coefficient * power_ratio(u, gap)
    return (
        up.reshape(8 * LANES, LANES).astype(np.float32),
        down.transpose(1, 0, 2).reshape(LANES, 8 * LANES).astype(np.float32),
    )


@functools.lru_cache(None)
def window_table():
    grid = [(x - 3, y - 3, z - 3) for x in range(7) for y in range(7) for z in range(7)]
    table = translation(grid).reshape(49, 7 * LANES, LANES).astype(np.float32)
    high = table.astype(ml_dtypes.bfloat16)
    low = (table - high.astype(np.float32)).astype(ml_dtypes.bfloat16)
    return np.concatenate([high, low], axis=-1)


@functools.lru_cache(None)
def top_table(shape):
    grid = [
        (x, y, z)
        for x in range(1 - shape[0], shape[0])
        for y in range(1 - shape[1], shape[1])
        for z in range(1 - shape[2], shape[2])
    ]
    table = translation(grid)[:, :, :]
    return table.reshape(tuple(2 * s - 1 for s in shape) + (LANES, LANES)).astype(np.float32)


def harmonics(position):
    ladders = []
    for d in range(3):
        rungs = [jnp.ones_like(position[d])]
        for step in range(1, ORDER + 1):
            rungs.append(rungs[-1] * position[d] * (1.0 / step))
        ladders.append(rungs)
    flat = {
        (a, b): ladders[0][a] * ladders[1][b] for a in range(ORDER + 1) for b in range(ORDER + 1 - a)
    }
    found = []
    for a, b, c in BASIS:
        total = None
        for w in range(a // 2 + b // 2 + 1):
            inner = None
            for u in range(w + 1):
                v = w - u
                if 2 * u <= a and 2 * v <= b:
                    term = flat[(a - 2 * u, b - 2 * v)]
                    factor = (-1.0) ** w * math.comb(w, u)
                    term = term if factor == 1.0 else term * factor
                    inner = term if inner is None else inner + term
            if inner is not None:
                part = inner * ladders[2][c + 2 * w]
                total = part if total is None else total + part
        found.append(total)
    return found


def moment_kernel(position_ref, charge_ref, out_ref):
    charge = charge_ref[...]
    values = harmonics([position_ref[d] - 0.5 for d in range(3)])
    lane = lax.broadcasted_iota(jnp.int32, (8, LANES), 1)
    total = jnp.zeros((8, LANES), jnp.float32)
    for h, n in enumerate(BASIS):
        summed = jnp.sum(values[h] * charge, axis=1, keepdims=True)
        if sum(n) % 2:
            summed = -summed
        total = jnp.where(lane == h, summed, total)
    out_ref[...] = total


def leaf_moments(offsets, charge):
    tiles, slots = charge.shape
    return pl.pallas_call(
        moment_kernel,
        grid=(tiles // 8,),
        out_shape=jax.ShapeDtypeStruct((tiles, LANES), jnp.float32),
        in_specs=[
            pl.BlockSpec((3, 8, slots), lambda i: (0, i, 0)),
            pl.BlockSpec((8, slots), lambda i: (i, 0)),
        ],
        out_specs=pl.BlockSpec((8, LANES), lambda i: (i, 0)),
        compiler_params=pltpu.CompilerParams(vmem_limit_bytes=VMEM_BYTES),
    )(offsets, charge)


def evaluate_kernel(position_ref, charge_ref, live_ref, near_ref, total_ref, leaf_ref, full_ref, part_ref, far_ref):
    live = live_ref[...]
    values = harmonics([position_ref[d] - 0.5 for d in range(3)])
    total, leaf = total_ref[...], leaf_ref[...]
    far = jnp.zeros_like(live)
    local = jnp.zeros_like(live)
    for h in range(TERMS):
        far = far + values[h] * total[:, h : h + 1]
        local = local + values[h] * leaf[:, h : h + 1]
    near = jnp.where(live > 0.0, near_ref[...] - charge_ref[...] / SOFTENING, 0.0)
    full_ref[...] = -(near + far) * live
    part_ref[...] = -near * live
    far_ref[...] = -local * live


def evaluate(offsets, charge, live, near, total, leaf):
    tiles, slots = charge.shape
    row = pl.BlockSpec((8, slots), lambda i: (i, 0))
    shape = jax.ShapeDtypeStruct((tiles, slots), jnp.float32)
    return pl.pallas_call(
        evaluate_kernel,
        grid=(tiles // 8,),
        out_shape=(shape, shape, shape),
        in_specs=[pl.BlockSpec((3, 8, slots), lambda i: (0, i, 0)), row, row, row, row, row],
        out_specs=(row, row, row),
        compiler_params=pltpu.CompilerParams(vmem_limit_bytes=VMEM_BYTES),
    )(offsets, charge, live, near, total, leaf)


def near_kernel(extents, counts_ref, window_ref, out_ref, columns_ref, sums_ref):
    lx, ly, lz = extents

    def one_leaf(leaf, carry):
        x = leaf // (ly * lz)
        y = lax.rem(leaf // lz, ly)
        z = lax.rem(leaf, lz)

        def cell(p, q, r):
            return ((x + p) * (ly + 2) + y + q) * (lz + 2) + z + r

        columns_ref[...] = jnp.transpose(window_ref[cell(1, 1, 1)])

        def one_chunk(chunk, inner):
            start = pl.multiple_of(chunk * ROWS, ROWS)
            target = columns_ref[pl.ds(start, ROWS), :]
            wide = [jnp.broadcast_to(target[:, d : d + 1], (ROWS, LANES)) for d in range(3)]
            moved = [[wide[d] - float(s - 1) for s in range(3)] for d in range(3)]
            total = jnp.zeros((ROWS, LANES), jnp.float32)
            for p in range(3):
                for q in range(3):
                    for r in range(3):
                        index = cell(p, q, r)
                        gx = window_ref[index, 0:1, :] - moved[0][p]
                        gy = window_ref[index, 1:2, :] - moved[1][q]
                        gz = window_ref[index, 2:3, :] - moved[2][r]
                        squared = (gx * gx + SOFTENING * SOFTENING) + (gy * gy + gz * gz)
                        total = total + window_ref[index, 3:4, :] * lax.rsqrt(squared)
            sums_ref[pl.ds(start, ROWS), :] = total
            return inner

        lax.fori_loop(0, (counts_ref[leaf] + ROWS - 1) // ROWS, one_chunk, 0)
        out_ref[pl.ds(leaf, 1), :] = jnp.sum(jnp.transpose(sums_ref[...]), axis=0, keepdims=True)
        return carry

    lax.fori_loop(0, lx * ly * lz, one_leaf, 0)


def near_field(window, counts, extents):
    tiles = extents[0] * extents[1] * extents[2]
    return pl.pallas_call(
        functools.partial(near_kernel, extents),
        out_shape=jax.ShapeDtypeStruct((tiles, LANES), jnp.float32),
        in_specs=[
            pl.BlockSpec(memory_space=pltpu.SMEM),
            pl.BlockSpec(memory_space=pltpu.VMEM),
        ],
        out_specs=pl.BlockSpec(memory_space=pltpu.VMEM),
        scratch_shapes=[
            pltpu.VMEM((LANES, 8), jnp.float32),
            pltpu.VMEM((LANES, LANES), jnp.float32),
        ],
        compiler_params=pltpu.CompilerParams(vmem_limit_bytes=VMEM_BYTES),
    )(counts, window)


def local_kernel(lx, plane, small, leaf_ref, mid_ref, table_ref, out_ref, acc_ref):
    step = pl.program_id(0)
    dx, dy = step // 7, lax.rem(step, 7)
    rows = lx * plane
    depth = 7 * LANES

    @pl.when(step == 0)
    def _():
        acc_ref[...] = jnp.zeros_like(acc_ref)

    leaf = leaf_ref[dy, pl.ds(dx, lx)].reshape(rows, depth)
    odd = lax.rem(lax.broadcasted_iota(jnp.int32, (rows, depth), 0) // plane, 2)
    drop = jnp.where(dx == 0, 0, jnp.where(dx == 6, 1, 2))
    leaf = jnp.where(odd == drop, 0.0, leaf)
    whole = jnp.concatenate([leaf, mid_ref[0]], axis=0)
    high = whole.astype(jnp.bfloat16).astype(jnp.float32)
    both = jnp.concatenate([high, whole - high], axis=0).astype(jnp.bfloat16)
    acc_ref[...] += jnp.dot(both, table_ref[0], preferred_element_type=jnp.float32)

    @pl.when(step == 48)
    def _():
        cut = rows + small
        out_ref[...] = (
            acc_ref[:cut, :LANES] + acc_ref[:cut, LANES:] + acc_ref[cut:, :LANES]
        )


def local_expansions(leaf, mid, table):
    lx, plane, depth = leaf.shape[1] - 6, leaf.shape[2], leaf.shape[3]
    small = mid.shape[1]
    rows = lx * plane + small
    return pl.pallas_call(
        functools.partial(local_kernel, lx, plane, small),
        grid=(49,),
        out_shape=jax.ShapeDtypeStruct((rows, LANES), jnp.float32),
        in_specs=[
            pl.BlockSpec(memory_space=pltpu.VMEM),
            pl.BlockSpec((1, small, depth), lambda i: (i, 0, 0)),
            pl.BlockSpec((1, depth, 2 * LANES), lambda i: (i, 0, 0)),
        ],
        out_specs=pl.BlockSpec((rows, LANES), lambda i: (0, 0)),
        scratch_shapes=[pltpu.VMEM((2 * rows, 2 * LANES), jnp.float32)],
        compiler_params=pltpu.CompilerParams(vmem_limit_bytes=VMEM_BYTES),
    )(leaf, mid, table)


def with_halo(shard, sides, width):
    for axis, dim in sides:
        peers, length = (lax.axis_size(axis), shard.shape[dim])
        up = [(i, (i + 1) % peers) for i in range(peers - 1)]
        down = [(j, i) for i, j in up]
        before = lax.ppermute(lax.slice_in_dim(shard, length - width, length, axis=dim), axis, up)
        after = lax.ppermute(lax.slice_in_dim(shard, 0, width, axis=dim), axis, down)
        shard = jnp.concatenate([before, shard, after], axis=dim)
    return shard


def gather_axis(piece, axis):
    peers, me = lax.axis_size(axis), lax.axis_index(axis)
    whole = jnp.zeros((peers,) + piece.shape, piece.dtype)
    rest = (0,) * piece.ndim
    whole = lax.dynamic_update_slice(whole, piece[None], (me,) + rest)
    for step in range(1, peers):
        came = lax.ppermute(piece, axis, [(i, (i + step) % peers) for i in range(peers)])
        whole = lax.dynamic_update_slice(whole, came[None], (lax.rem(me + peers - step, peers),) + rest)
    return whole


def kept(length, shift):
    cells = np.arange(length)
    return (np.abs((cells + shift - 3) // 2 - cells // 2) <= 1).astype(np.float32)


def side_by_side(window, length):
    return jnp.concatenate(
        [window[:, :, s : s + length] * kept(length, s)[:, None] for s in range(7)], axis=-1
    )


def group(moments):
    a, b, c, n = moments.shape
    paired = moments.reshape(a // 2, 2, b // 2, 2, c // 2, 2, n).transpose(0, 2, 4, 1, 3, 5, 6)
    return paired.reshape(a * b * c // 8, 8 * n)


def spread(parents, extents):
    a, b, c = extents
    apart = parents.reshape(a, b, c, 2, 2, 2, LANES).transpose(0, 3, 1, 4, 2, 5, 6)
    return apart.reshape(8 * a * b * c, LANES)


def shards(offsets, masses, counts):
    lx, ly, lz = counts.shape
    slots = masses.shape[-1]
    tiles = lx * ly * lz
    live = (jnp.arange(slots, dtype=jnp.int32)[None, None, None, :] < counts[..., None]).astype(
        jnp.float32
    )
    charge = masses * live
    flat_offsets = offsets.reshape(3, tiles, slots)
    flat_charge, flat_live = charge.reshape(tiles, slots), live.reshape(tiles, slots)

    moments0 = leaf_moments(flat_offsets, flat_charge).reshape(lx, ly, lz, LANES)
    up, down = shift_tables()
    mid = (lx // 2, ly // 2, lz // 2)
    top = (lx // 4, ly // 4, lz // 4)
    moments1 = jnp.dot(group(moments0), up, precision=HIGHEST)
    moments2 = jnp.dot(group(moments1.reshape(mid + (LANES,))), up, precision=HIGHEST)
    n_mid, n_top = moments1.shape[0], moments2.shape[0]

    pieces = jnp.concatenate([moments1, moments2], axis=0)
    for axis in ("gz", "gy", "gx"):
        pieces = gather_axis(pieces, axis)
    span = pieces.shape[:3]
    place = tuple(lax.axis_index(axis) for axis in ("gx", "gy", "gz"))

    def whole_grid(part, extents):
        shaped = part.reshape(span + extents + (LANES,)).transpose(0, 3, 1, 4, 2, 5, 6)
        return shaped.reshape(tuple(span[i] * extents[i] for i in range(3)) + (LANES,))

    whole1 = whole_grid(pieces[:, :, :, :n_mid], mid)
    whole2 = whole_grid(pieces[:, :, :, n_mid:], top)

    packed = jnp.stack([offsets[0], offsets[1], offsets[2], charge], axis=3)
    packed = with_halo(packed, (("gx", 0), ("gy", 1), ("gz", 2)), 1)
    packed = jnp.pad(packed, ((0, 0),) * 3 + ((0, 4), (0, 0)))
    near = near_field(packed.reshape(-1, 8, slots), counts.reshape(-1), (lx, ly, lz))

    window0 = with_halo(moments0, (("gx", 0), ("gy", 1), ("gz", 2)), 3)
    lined = side_by_side(window0, lz)
    lined = jnp.stack(
        [lined[:, s : s + ly] * kept(ly, s)[:, None, None] for s in range(7)]
    ).reshape(7, lx + 6, ly * lz, 7 * LANES)
    padded1 = jnp.pad(whole1, ((3, 3), (3, 3), (3, 3), (0, 0)))
    window1 = lax.dynamic_slice(
        padded1,
        tuple(place[i] * mid[i] for i in range(3)) + (0,),
        tuple(mid[i] + 6 for i in range(3)) + (LANES,),
    )
    lined1 = side_by_side(window1, mid[2])
    mids = jnp.stack(
        [
            lined1[s : s + mid[0], t : t + mid[1]]
            * (kept(mid[0], s)[:, None] * kept(mid[1], t)[None, :])[:, :, None, None]
            for s in range(7)
            for t in range(7)
        ]
    ).reshape(49, n_mid, 7 * LANES)
    locals01 = local_expansions(lined, mids, jnp.asarray(window_table()))
    local0, local1 = locals01[:tiles], 0.5 * locals01[tiles:]

    grid2 = whole2.shape[:3]
    table2 = jnp.asarray(top_table(grid2))
    rows2 = []
    for a in range(top[0]):
        for b in range(top[1]):
            for c in range(top[2]):
                start = tuple(
                    grid2[i] - 1 - (place[i] * top[i] + (a, b, c)[i]) for i in range(3)
                )
                used = lax.dynamic_slice(table2, start + (0, 0), grid2 + (LANES, LANES))
                rows2.append(
                    jnp.sum(whole2[..., :, None] * used, axis=(0, 1, 2, 3))
                )
    local2 = 0.25 * jnp.stack(rows2)
    total1 = local1 + spread(jnp.dot(local2, down, precision=HIGHEST), top)
    total0 = local0 + spread(jnp.dot(total1, down, precision=HIGHEST), mid)

    outs = evaluate(flat_offsets, flat_charge, flat_live, near, total0, local0)
    return tuple(out.reshape(lx, ly, lz, slots) for out in outs)


def solution(mesh):
    placed = (P(None, "gx", "gy", "gz", None), P("gx", "gy", "gz", None), P("gx", "gy", "gz"))
    return jax.shard_map(
        shards,
        mesh=mesh,
        in_specs=placed,
        out_specs=(P("gx", "gy", "gz", None),) * 3,
        check_vma=False,
    )
```

```python
import functools
import math

import jax
import jax.numpy as jnp
import ml_dtypes
import numpy as np
from jax import lax
from jax.experimental import pallas as pl
from jax.experimental.pallas import tpu as pltpu
from jax.sharding import PartitionSpec as P

ORDER = 8
SOFTENING = 0.02
HIGHEST = lax.Precision.HIGHEST
LANES = 128
ROWS = 16
VMEM_BYTES = 48 * 1024 * 1024


def multi_indices():
    listed = []
    for degree in range(ORDER + 1):
        for first in range(degree, -1, -1):
            for second in range(degree - first, -1, -1):
                listed.append((first, second, degree - first - second))
    return listed


FULL = multi_indices()
BASIS = [n for n in FULL if n[2] <= 1]
SLOT = {n: i for i, n in enumerate(BASIS)}
TERMS = len(BASIS)


def fold_row(n):
    w = n[2] // 2
    return [
        (SLOT[(n[0] + 2 * u, n[1] + 2 * (w - u), n[2] - 2 * w)], (-1.0) ** w * math.comb(w, u))
        for u in range(w + 1)
    ]


def derivatives(vectors):
    r = [vectors[:, i] for i in range(3)]
    sq = r[0] ** 2 + r[1] ** 2 + r[2] ** 2
    a = {(0, 0, 0): 1.0 / np.sqrt(sq)}
    for n in FULL[1:]:
        d = sum(n)
        lin = np.zeros_like(sq)
        two = np.zeros_like(sq)
        for i in range(3):
            low = list(n)
            low[i] -= 1
            if low[i] >= 0:
                lin = lin + r[i] * a[tuple(low)]
            low[i] -= 1
            if low[i] >= 0:
                two = two + a[tuple(low)]
        a[n] = -((2 * d - 1) * lin + (d - 1) * two) / (d * sq)
    return {n: a[n] * math.prod(math.factorial(c) for c in n) for n in FULL}


def translation(offsets):
    offsets = np.asarray(offsets, np.float64)
    near = np.max(np.abs(offsets), axis=1) <= 1.5
    b = derivatives(np.where(near[:, None], [4.0, 0.0, 0.0], -offsets))
    out = np.zeros((len(offsets), LANES, LANES))
    for h, hn in enumerate(BASIS):
        for j, jn in enumerate(BASIS):
            n = tuple(hn[i] + jn[i] for i in range(3))
            if sum(n) <= ORDER:
                out[:, h, j] = np.where(near, 0.0, b[n])
    return out


def power_ratio(u, k):
    if min(k) < 0:
        return 0.0
    return math.prod(u[i] ** k[i] / math.factorial(k[i]) for i in range(3))


@functools.lru_cache(None)
def shift_tables():
    up = np.zeros((8, LANES, LANES))
    down = np.zeros((8, LANES, LANES))
    for g in range(8):
        u = [(g >> 2 & 1) - 0.5, (g >> 1 & 1) - 0.5, (g & 1) - 0.5]
        for n in FULL:
            scale = 0.5 ** sum(n)
            for h, coefficient in fold_row(n):
                for i, k in enumerate(BASIS):
                    gap = tuple(n[d] - k[d] for d in range(3))
                    up[g, i, h] += scale * coefficient * power_ratio([-c for c in u], gap)
                    down[g, h, i] += scale * coefficient * power_ratio(u, gap)
    return (
        up.reshape(8 * LANES, LANES).astype(np.float32),
        down.transpose(1, 0, 2).reshape(LANES, 8 * LANES).astype(np.float32),
    )


@functools.lru_cache(None)
def window_table():
    grid = [(x - 3, y - 3, z - 3) for x in range(7) for y in range(7) for z in range(7)]
    table = translation(grid).reshape(49, 7 * LANES, LANES).astype(np.float32)
    high = table.astype(ml_dtypes.bfloat16)
    low = (table - high.astype(np.float32)).astype(ml_dtypes.bfloat16)
    return np.concatenate([high, low], axis=-1)


@functools.lru_cache(None)
def top_table(shape):
    grid = [
        (x, y, z)
        for x in range(1 - shape[0], shape[0])
        for y in range(1 - shape[1], shape[1])
        for z in range(1 - shape[2], shape[2])
    ]
    table = translation(grid)[:, :, :]
    return table.reshape(tuple(2 * s - 1 for s in shape) + (LANES, LANES)).astype(np.float32)


def harmonics(position):
    ladders = []
    for d in range(3):
        rungs = [jnp.ones_like(position[d])]
        for step in range(1, ORDER + 1):
            rungs.append(rungs[-1] * position[d] * (1.0 / step))
        ladders.append(rungs)
    flat = {
        (a, b): ladders[0][a] * ladders[1][b] for a in range(ORDER + 1) for b in range(ORDER + 1 - a)
    }
    found = []
    for a, b, c in BASIS:
        total = None
        for w in range(a // 2 + b // 2 + 1):
            inner = None
            for u in range(w + 1):
                v = w - u
                if 2 * u <= a and 2 * v <= b:
                    term = flat[(a - 2 * u, b - 2 * v)]
                    factor = (-1.0) ** w * math.comb(w, u)
                    term = term if factor == 1.0 else term * factor
                    inner = term if inner is None else inner + term
            if inner is not None:
                part = inner * ladders[2][c + 2 * w]
                total = part if total is None else total + part
        found.append(total)
    return found


def moment_kernel(position_ref, charge_ref, out_ref):
    charge = charge_ref[...]
    values = harmonics([position_ref[d] - 0.5 for d in range(3)])
    lane = lax.broadcasted_iota(jnp.int32, (8, LANES), 1)
    total = jnp.zeros((8, LANES), jnp.float32)
    for h, n in enumerate(BASIS):
        summed = jnp.sum(values[h] * charge, axis=1, keepdims=True)
        if sum(n) % 2:
            summed = -summed
        total = jnp.where(lane == h, summed, total)
    out_ref[...] = total


def leaf_moments(offsets, charge):
    tiles, slots = charge.shape
    return pl.pallas_call(
        moment_kernel,
        grid=(tiles // 8,),
        out_shape=jax.ShapeDtypeStruct((tiles, LANES), jnp.float32),
        in_specs=[
            pl.BlockSpec((3, 8, slots), lambda i: (0, i, 0)),
            pl.BlockSpec((8, slots), lambda i: (i, 0)),
        ],
        out_specs=pl.BlockSpec((8, LANES), lambda i: (i, 0)),
        compiler_params=pltpu.CompilerParams(vmem_limit_bytes=VMEM_BYTES),
    )(offsets, charge)


def evaluate_kernel(position_ref, charge_ref, live_ref, near_ref, total_ref, leaf_ref, full_ref, part_ref, far_ref):
    live = live_ref[...]
    values = harmonics([position_ref[d] - 0.5 for d in range(3)])
    total, leaf = total_ref[...], leaf_ref[...]
    far = jnp.zeros_like(live)
    local = jnp.zeros_like(live)
    for h in range(TERMS):
        far = far + values[h] * total[:, h : h + 1]
        local = local + values[h] * leaf[:, h : h + 1]
    near = jnp.where(live > 0.0, near_ref[...] - charge_ref[...] / SOFTENING, 0.0)
    full_ref[...] = -(near + far) * live
    part_ref[...] = -near * live
    far_ref[...] = -local * live


def evaluate(offsets, charge, live, near, total, leaf):
    tiles, slots = charge.shape
    row = pl.BlockSpec((8, slots), lambda i: (i, 0))
    shape = jax.ShapeDtypeStruct((tiles, slots), jnp.float32)
    return pl.pallas_call(
        evaluate_kernel,
        grid=(tiles // 8,),
        out_shape=(shape, shape, shape),
        in_specs=[pl.BlockSpec((3, 8, slots), lambda i: (0, i, 0)), row, row, row, row, row],
        out_specs=(row, row, row),
        compiler_params=pltpu.CompilerParams(vmem_limit_bytes=VMEM_BYTES),
    )(offsets, charge, live, near, total, leaf)


def near_kernel(extents, counts_ref, window_ref, out_ref, columns_ref, sums_ref):
    lx, ly, lz = extents

    def one_leaf(leaf, carry):
        x = leaf // (ly * lz)
        y = lax.rem(leaf // lz, ly)
        z = lax.rem(leaf, lz)

        def cell(p, q, r):
            return ((x + p) * (ly + 2) + y + q) * (lz + 2) + z + r

        def one_chunk(chunk, inner):
            start = pl.multiple_of(chunk * ROWS, ROWS)
            target = columns_ref[leaf, pl.ds(start, ROWS), :]
            wide = [jnp.broadcast_to(target[:, d : d + 1], (ROWS, LANES)) for d in range(3)]
            moved = [[wide[d] - float(s - 1) for s in range(3)] for d in range(3)]
            total = jnp.zeros((ROWS, LANES), jnp.float32)
            for p in range(3):
                for q in range(3):
                    for r in range(3):
                        index = cell(p, q, r)
                        gx = window_ref[index, 0:1, :] - moved[0][p]
                        gy = window_ref[index, 1:2, :] - moved[1][q]
                        gz = window_ref[index, 2:3, :] - moved[2][r]
                        squared = (gx * gx + SOFTENING * SOFTENING) + (gy * gy + gz * gz)
                        total = total + window_ref[index, 3:4, :] * lax.rsqrt(squared)
            sums_ref[leaf, pl.ds(start, ROWS), :] = total
            return inner

        lax.fori_loop(0, (counts_ref[leaf] + ROWS - 1) // ROWS, one_chunk, 0)
        return carry

    def one_row(row, carry):
        first = ((row // ly + 1) * (ly + 2) + lax.rem(row, ly) + 1) * (lz + 2) + 1
        for z in range(lz):
            columns_ref[row * lz + z] = jnp.transpose(window_ref[first + z])
        return carry

    def one_group(number, carry):
        start = pl.multiple_of(number * 8, 8)
        summed = [
            jnp.sum(jnp.transpose(sums_ref[start + k]), axis=0, keepdims=True) for k in range(8)
        ]
        out_ref[pl.ds(start, 8), :] = jnp.concatenate(summed, axis=0)
        return carry

    lax.fori_loop(0, lx * ly, one_row, 0)
    lax.fori_loop(0, lx * ly * lz, one_leaf, 0)
    lax.fori_loop(0, lx * ly * lz // 8, one_group, 0)


def near_field(window, counts, extents):
    tiles = extents[0] * extents[1] * extents[2]
    return pl.pallas_call(
        functools.partial(near_kernel, extents),
        out_shape=jax.ShapeDtypeStruct((tiles, LANES), jnp.float32),
        in_specs=[
            pl.BlockSpec(memory_space=pltpu.SMEM),
            pl.BlockSpec(memory_space=pltpu.VMEM),
        ],
        out_specs=pl.BlockSpec(memory_space=pltpu.VMEM),
        scratch_shapes=[
            pltpu.VMEM((tiles, LANES, 8), jnp.float32),
            pltpu.VMEM((tiles, LANES, LANES), jnp.float32),
        ],
        compiler_params=pltpu.CompilerParams(vmem_limit_bytes=VMEM_BYTES),
    )(counts, window)


def local_kernel(extents, leaf_ref, mid_ref, table_ref, out_ref, lined_ref, mids_ref, acc_ref):
    step = pl.program_id(0)
    dx, dy = step // 7, lax.rem(step, 7)
    lx, ly, lz = extents
    mx, my, mz = (e // 2 for e in extents)
    plane = ly * lz
    rows, small, depth = lx * plane, mx * my * mz, 7 * LANES

    def stays(length, shift, cell):
        return kept(length, shift)[cell] > 0.0

    @pl.when(step == 0)
    def _():
        acc_ref[...] = jnp.zeros_like(acc_ref)
        nothing = jnp.zeros((1, LANES), jnp.float32)

        def one_plane(x, carry):
            for t in range(7):
                for y in range(ly):
                    for z in range(lz):
                        for s in range(7):
                            lanes = slice(s * LANES, (s + 1) * LANES)
                            good = stays(ly, t, y) and stays(lz, s, z)
                            row = y * lz + z
                            value = leaf_ref[x, y + t, z + s] if good else nothing
                            lined_ref[t, x, row : row + 1, lanes] = value
            return carry

        lax.fori_loop(0, lx + 6, one_plane, 0)

        def one_shift(r, carry):
            for t in range(7):
                for x in range(mx):
                    for y in range(my):
                        for z in range(mz):
                            for s in range(7):
                                lanes = slice(s * LANES, (s + 1) * LANES)
                                good = stays(my, t, y) and stays(mz, s, z)
                                row = (x * my + y) * mz + z
                                value = mid_ref[x + r, y + t, z + s] if good else nothing
                                mids_ref[r * 7 + t, row : row + 1, lanes] = value
            return carry

        lax.fori_loop(0, 7, one_shift, 0)

    drop = jnp.where(dx == 0, 0, jnp.where(dx == 6, 1, 2))

    def masked(value, stride):
        odd = lax.rem(lax.broadcasted_iota(jnp.int32, value.shape, 0) // stride, 2)
        return jnp.where(odd == drop, 0.0, value)

    leaf = masked(lined_ref[dy, pl.ds(dx, lx)].reshape(rows, depth), plane)
    whole = jnp.concatenate([leaf, masked(mids_ref[step], my * mz)], axis=0)
    high = whole.astype(jnp.bfloat16).astype(jnp.float32)
    both = jnp.concatenate([high, whole - high], axis=0).astype(jnp.bfloat16)
    acc_ref[...] += jnp.dot(both, table_ref[0], preferred_element_type=jnp.float32)

    @pl.when(step == 48)
    def _():
        cut = rows + small
        out_ref[...] = (
            acc_ref[:cut, :LANES] + acc_ref[:cut, LANES:] + acc_ref[cut:, :LANES]
        )


def local_expansions(leaf, mid, table, extents):
    lx, ly, lz = extents
    small = lx * ly * lz // 8
    rows, depth = lx * ly * lz + small, 7 * LANES
    return pl.pallas_call(
        functools.partial(local_kernel, extents),
        grid=(49,),
        out_shape=jax.ShapeDtypeStruct((rows, LANES), jnp.float32),
        in_specs=[
            pl.BlockSpec(memory_space=pltpu.VMEM),
            pl.BlockSpec(memory_space=pltpu.VMEM),
            pl.BlockSpec((1, depth, 2 * LANES), lambda i: (i, 0, 0)),
        ],
        out_specs=pl.BlockSpec((rows, LANES), lambda i: (0, 0)),
        scratch_shapes=[
            pltpu.VMEM((7, lx + 6, ly * lz, depth), jnp.float32),
            pltpu.VMEM((49, small, depth), jnp.float32),
            pltpu.VMEM((2 * rows, 2 * LANES), jnp.float32),
        ],
        compiler_params=pltpu.CompilerParams(vmem_limit_bytes=VMEM_BYTES),
    )(leaf, mid, table)


AXES = ("gx", "gy", "gz")


def exchange_kernel(sizes, moments_ref, packed_ref, upper_ref, window_ref, near_ref, whole_ref, send_sem, recv_sem, far_send, far_recv):
    place = [lax.axis_index(axis) for axis in AXES]
    window_ref[...] = jnp.zeros_like(window_ref)
    near_ref[...] = jnp.zeros_like(near_ref)
    lx, ly, lz = moments_ref.shape[:3]
    window_ref[3 : 3 + lx, 3 : 3 + ly, 3 : 3 + lz] = moments_ref[...]
    near_ref[1 : 1 + lx, 1 : 1 + ly, 1 : 1 + lz] = packed_ref[...]
    whole_ref[place[0], place[1], place[2]] = upper_ref[...]

    barrier = pltpu.get_barrier_semaphore()
    for d, axis in enumerate(AXES):
        for step in range(1, sizes[d]):
            peer = lax.rem(place[d] + step, sizes[d])
            pl.semaphore_signal(
                barrier, inc=1, device_id={axis: peer}, device_id_type=pl.DeviceIdType.MESH
            )
    pl.semaphore_wait(barrier, sum(sizes) - 3)

    slot = 0
    for d, axis in enumerate(AXES):
        n, me = sizes[d], place[d]
        ups, downs, shares, arrivals = [], [], [], []
        for k, (ref, width) in enumerate(((window_ref, 3), (near_ref, 1))):
            length = moments_ref.shape[d]

            def part(start):
                later = tuple(pl.ds(width, extent) for extent in moments_ref.shape[d + 1 : 3])
                return ref.at[(slice(None),) * d + (pl.ds(start, width),) + later]

            for way, (source, target) in enumerate(((length, 0), (width, length + width))):
                copy = pltpu.make_async_remote_copy(
                    src_ref=part(source),
                    dst_ref=part(target),
                    send_sem=send_sem.at[d * 4 + k * 2 + way],
                    recv_sem=recv_sem.at[d * 4 + k * 2 + way],
                    device_id={axis: me + 1 - 2 * way},
                    device_id_type=pl.DeviceIdType.MESH,
                )
                (ups, downs)[way].append(copy)

        def share(index, step, peer):
            ref = whole_ref.at[(slice(None),) * d + (index,) + tuple(place[d + 1 :])]
            return pltpu.make_async_remote_copy(
                src_ref=ref,
                dst_ref=ref,
                send_sem=far_send.at[slot + step - 1],
                recv_sem=far_recv.at[slot + step - 1],
                device_id={axis: peer},
                device_id_type=pl.DeviceIdType.MESH,
            )

        for step in range(1, n):
            peer = lax.rem(me + step, n)
            shares.append(share(me, step, peer))
            arrivals.append(share(lax.rem(me + n - step, n), step, peer))
        slot += n - 1

        @pl.when(me < n - 1)
        def _():
            for copy in ups:
                copy.start()

        @pl.when(me > 0)
        def _():
            for copy in downs:
                copy.start()

        for copy in shares:
            copy.start()

        @pl.when(me < n - 1)
        def _():
            for copy in ups:
                copy.wait_send()
            for copy in downs:
                copy.wait_recv()

        @pl.when(me > 0)
        def _():
            for copy in downs:
                copy.wait_send()
            for copy in ups:
                copy.wait_recv()

        for sent, came in zip(shares, arrivals):
            sent.wait_send()
            came.wait_recv()


def exchange(moments, packed, upper):
    sizes = tuple(lax.axis_size(axis) for axis in AXES)
    lx, ly, lz = moments.shape[:3]
    steps = sum(sizes) - 3
    full = pl.BlockSpec(memory_space=pltpu.VMEM)
    return pl.pallas_call(
        functools.partial(exchange_kernel, sizes),
        out_shape=(
            jax.ShapeDtypeStruct((lx + 6, ly + 6, lz + 6, 1, LANES), jnp.float32),
            jax.ShapeDtypeStruct((lx + 2, ly + 2, lz + 2, 8, LANES), jnp.float32),
            jax.ShapeDtypeStruct(sizes + upper.shape, jnp.float32),
        ),
        in_specs=[full] * 3,
        out_specs=(full,) * 3,
        scratch_shapes=[
            pltpu.SemaphoreType.DMA((12,)),
            pltpu.SemaphoreType.DMA((12,)),
            pltpu.SemaphoreType.DMA((steps,)),
            pltpu.SemaphoreType.DMA((steps,)),
        ],
        compiler_params=pltpu.CompilerParams(
            collective_id=0, has_side_effects=True, vmem_limit_bytes=VMEM_BYTES
        ),
    )(moments, packed, upper)


def kept(length, shift):
    cells = np.arange(length)
    return (np.abs((cells + shift - 3) // 2 - cells // 2) <= 1).astype(np.float32)


def group(moments):
    a, b, c, n = moments.shape
    paired = moments.reshape(a // 2, 2, b // 2, 2, c // 2, 2, n).transpose(0, 2, 4, 1, 3, 5, 6)
    return paired.reshape(a * b * c // 8, 8 * n)


def spread(parents, extents):
    a, b, c = extents
    apart = parents.reshape(a, b, c, 2, 2, 2, LANES).transpose(0, 3, 1, 4, 2, 5, 6)
    return apart.reshape(8 * a * b * c, LANES)


def shards(offsets, masses, counts):
    lx, ly, lz = counts.shape
    slots = masses.shape[-1]
    tiles = lx * ly * lz
    live = (jnp.arange(slots, dtype=jnp.int32)[None, None, None, :] < counts[..., None]).astype(
        jnp.float32
    )
    charge = masses * live
    flat_offsets = offsets.reshape(3, tiles, slots)
    flat_charge, flat_live = charge.reshape(tiles, slots), live.reshape(tiles, slots)

    moments0 = leaf_moments(flat_offsets, flat_charge).reshape(lx, ly, lz, LANES)
    up, down = shift_tables()
    mid = (lx // 2, ly // 2, lz // 2)
    top = (lx // 4, ly // 4, lz // 4)
    moments1 = jnp.dot(group(moments0), up, precision=HIGHEST)
    moments2 = jnp.dot(group(moments1.reshape(mid + (LANES,))), up, precision=HIGHEST)
    n_mid, n_top = moments1.shape[0], moments2.shape[0]

    upper = jnp.concatenate([moments1, moments2], axis=0)
    upper = jnp.pad(upper, ((0, -upper.shape[0] % 8), (0, 0)))
    blank = jnp.zeros_like(charge)
    packed = jnp.stack([offsets[0], offsets[1], offsets[2], charge] + [blank] * 4, axis=3)
    window0, near_window, pieces = exchange(moments0[:, :, :, None], packed, upper)
    span = pieces.shape[:3]
    place = tuple(lax.axis_index(axis) for axis in ("gx", "gy", "gz"))

    def whole_grid(part, extents):
        shaped = part.reshape(span + extents + (LANES,)).transpose(0, 3, 1, 4, 2, 5, 6)
        return shaped.reshape(tuple(span[i] * extents[i] for i in range(3)) + (LANES,))

    whole1 = whole_grid(pieces[:, :, :, :n_mid], mid)
    whole2 = whole_grid(pieces[:, :, :, n_mid : n_mid + n_top], top)

    near = near_field(near_window.reshape(-1, 8, slots), counts.reshape(-1), (lx, ly, lz))
    padded1 = jnp.pad(whole1, ((3, 3), (3, 3), (3, 3), (0, 0)))
    window1 = lax.dynamic_slice(
        padded1,
        tuple(place[i] * mid[i] for i in range(3)) + (0,),
        tuple(mid[i] + 6 for i in range(3)) + (LANES,),
    )
    locals01 = local_expansions(
        window0, window1[:, :, :, None], jnp.asarray(window_table()), (lx, ly, lz)
    )
    local0, local1 = locals01[:tiles], 0.5 * locals01[tiles:]

    grid2 = whole2.shape[:3]
    table2 = jnp.asarray(top_table(grid2))
    rows2 = []
    for a in range(top[0]):
        for b in range(top[1]):
            for c in range(top[2]):
                start = tuple(
                    grid2[i] - 1 - (place[i] * top[i] + (a, b, c)[i]) for i in range(3)
                )
                used = lax.dynamic_slice(table2, start + (0, 0), grid2 + (LANES, LANES))
                rows2.append(
                    jnp.sum(whole2[..., :, None] * used, axis=(0, 1, 2, 3))
                )
    local2 = 0.25 * jnp.stack(rows2)
    total1 = local1 + spread(jnp.dot(local2, down, precision=HIGHEST), top)
    total0 = local0 + spread(jnp.dot(total1, down, precision=HIGHEST), mid)

    outs = evaluate(flat_offsets, flat_charge, flat_live, near, total0, local0)
    return tuple(out.reshape(lx, ly, lz, slots) for out in outs)


def solution(mesh):
    placed = (P(None, "gx", "gy", "gz", None), P("gx", "gy", "gz", None), P("gx", "gy", "gz"))
    return jax.shard_map(
        shards,
        mesh=mesh,
        in_specs=placed,
        out_specs=(P("gx", "gy", "gz", None),) * 3,
        check_vma=False,
    )
```

```python
import functools
import math

import jax
import jax.numpy as jnp
import ml_dtypes
import numpy as np
from jax import lax
from jax.experimental import pallas as pl
from jax.experimental.pallas import tpu as pltpu
from jax.sharding import PartitionSpec as P

ORDER = 8
SOFTENING = 0.02
HIGHEST = lax.Precision.HIGHEST
LANES = 128
ROWS = 32
VMEM_BYTES = 48 * 1024 * 1024


def multi_indices():
    listed = []
    for degree in range(ORDER + 1):
        for first in range(degree, -1, -1):
            for second in range(degree - first, -1, -1):
                listed.append((first, second, degree - first - second))
    return listed


FULL = multi_indices()
BASIS = [n for n in FULL if n[2] <= 1]
SLOT = {n: i for i, n in enumerate(BASIS)}
TERMS = len(BASIS)


def fold_row(n):
    w = n[2] // 2
    return [
        (SLOT[(n[0] + 2 * u, n[1] + 2 * (w - u), n[2] - 2 * w)], (-1.0) ** w * math.comb(w, u))
        for u in range(w + 1)
    ]


def derivatives(vectors):
    r = [vectors[:, i] for i in range(3)]
    sq = r[0] ** 2 + r[1] ** 2 + r[2] ** 2
    a = {(0, 0, 0): 1.0 / np.sqrt(sq)}
    for n in FULL[1:]:
        d = sum(n)
        lin = np.zeros_like(sq)
        two = np.zeros_like(sq)
        for i in range(3):
            low = list(n)
            low[i] -= 1
            if low[i] >= 0:
                lin = lin + r[i] * a[tuple(low)]
            low[i] -= 1
            if low[i] >= 0:
                two = two + a[tuple(low)]
        a[n] = -((2 * d - 1) * lin + (d - 1) * two) / (d * sq)
    return {n: a[n] * math.prod(math.factorial(c) for c in n) for n in FULL}


def translation(offsets):
    offsets = np.asarray(offsets, np.float64)
    near = np.max(np.abs(offsets), axis=1) <= 1.5
    b = derivatives(np.where(near[:, None], [4.0, 0.0, 0.0], -offsets))
    out = np.zeros((len(offsets), LANES, LANES))
    for h, hn in enumerate(BASIS):
        for j, jn in enumerate(BASIS):
            n = tuple(hn[i] + jn[i] for i in range(3))
            if sum(n) <= ORDER:
                out[:, h, j] = np.where(near, 0.0, b[n])
    return out


def power_ratio(u, k):
    if min(k) < 0:
        return 0.0
    return math.prod(u[i] ** k[i] / math.factorial(k[i]) for i in range(3))


@functools.lru_cache(None)
def shift_tables():
    up = np.zeros((8, LANES, LANES))
    down = np.zeros((8, LANES, LANES))
    for g in range(8):
        u = [(g >> 2 & 1) - 0.5, (g >> 1 & 1) - 0.5, (g & 1) - 0.5]
        for n in FULL:
            scale = 0.5 ** sum(n)
            for h, coefficient in fold_row(n):
                for i, k in enumerate(BASIS):
                    gap = tuple(n[d] - k[d] for d in range(3))
                    up[g, i, h] += scale * coefficient * power_ratio([-c for c in u], gap)
                    down[g, h, i] += scale * coefficient * power_ratio(u, gap)
    return (
        up.reshape(8 * LANES, LANES).astype(np.float32),
        down.transpose(1, 0, 2).reshape(LANES, 8 * LANES).astype(np.float32),
    )


@functools.lru_cache(None)
def window_table():
    grid = [(x - 3, y - 3, z - 3) for x in range(7) for y in range(7) for z in range(7)]
    table = translation(grid).reshape(49, 7 * LANES, LANES).astype(np.float32)
    high = table.astype(ml_dtypes.bfloat16)
    low = (table - high.astype(np.float32)).astype(ml_dtypes.bfloat16)
    return np.concatenate([high, low], axis=-1)


@functools.lru_cache(None)
def top_table(shape):
    grid = [
        (x, y, z)
        for x in range(1 - shape[0], shape[0])
        for y in range(1 - shape[1], shape[1])
        for z in range(1 - shape[2], shape[2])
    ]
    table = translation(grid)[:, :, :]
    return table.reshape(tuple(2 * s - 1 for s in shape) + (LANES, LANES)).astype(np.float32)


def harmonics(position):
    ladders = []
    for d in range(3):
        rungs = [jnp.ones_like(position[d])]
        for step in range(1, ORDER + 1):
            rungs.append(rungs[-1] * position[d] * (1.0 / step))
        ladders.append(rungs)
    flat = {
        (a, b): ladders[0][a] * ladders[1][b] for a in range(ORDER + 1) for b in range(ORDER + 1 - a)
    }
    found = []
    for a, b, c in BASIS:
        total = None
        for w in range(a // 2 + b // 2 + 1):
            inner = None
            for u in range(w + 1):
                v = w - u
                if 2 * u <= a and 2 * v <= b:
                    term = flat[(a - 2 * u, b - 2 * v)]
                    factor = (-1.0) ** w * math.comb(w, u)
                    term = term if factor == 1.0 else term * factor
                    inner = term if inner is None else inner + term
            if inner is not None:
                part = inner * ladders[2][c + 2 * w]
                total = part if total is None else total + part
        found.append(total)
    return found


def moment_kernel(position_ref, charge_ref, out_ref):
    charge = charge_ref[...]
    values = harmonics([position_ref[d] - 0.5 for d in range(3)])
    lane = lax.broadcasted_iota(jnp.int32, (8, LANES), 1)
    total = jnp.zeros((8, LANES), jnp.float32)
    for h, n in enumerate(BASIS):
        summed = jnp.sum(values[h] * charge, axis=1, keepdims=True)
        if sum(n) % 2:
            summed = -summed
        total = jnp.where(lane == h, summed, total)
    out_ref[...] = total


def leaf_moments(offsets, charge):
    tiles, slots = charge.shape
    return pl.pallas_call(
        moment_kernel,
        grid=(tiles // 8,),
        out_shape=jax.ShapeDtypeStruct((tiles, LANES), jnp.float32),
        in_specs=[
            pl.BlockSpec((3, 8, slots), lambda i: (0, i, 0)),
            pl.BlockSpec((8, slots), lambda i: (i, 0)),
        ],
        out_specs=pl.BlockSpec((8, LANES), lambda i: (i, 0)),
        compiler_params=pltpu.CompilerParams(vmem_limit_bytes=VMEM_BYTES),
    )(offsets, charge)


def evaluate_kernel(position_ref, charge_ref, live_ref, near_ref, total_ref, leaf_ref, full_ref, part_ref, far_ref):
    live = live_ref[...]
    values = harmonics([position_ref[d] - 0.5 for d in range(3)])
    total, leaf = total_ref[...], leaf_ref[...]
    far = jnp.zeros_like(live)
    local = jnp.zeros_like(live)
    for h in range(TERMS):
        far = far + values[h] * total[:, h : h + 1]
        local = local + values[h] * leaf[:, h : h + 1]
    near = jnp.where(live > 0.0, near_ref[...] - charge_ref[...] / SOFTENING, 0.0)
    full_ref[...] = -(near + far) * live
    part_ref[...] = -near * live
    far_ref[...] = -local * live


def evaluate(offsets, charge, live, near, total, leaf):
    tiles, slots = charge.shape
    row = pl.BlockSpec((8, slots), lambda i: (i, 0))
    shape = jax.ShapeDtypeStruct((tiles, slots), jnp.float32)
    return pl.pallas_call(
        evaluate_kernel,
        grid=(tiles // 8,),
        out_shape=(shape, shape, shape),
        in_specs=[pl.BlockSpec((3, 8, slots), lambda i: (0, i, 0)), row, row, row, row, row],
        out_specs=(row, row, row),
        compiler_params=pltpu.CompilerParams(vmem_limit_bytes=VMEM_BYTES),
    )(offsets, charge, live, near, total, leaf)


def near_kernel(extents, counts_ref, window_ref, out_ref, columns_ref, sums_ref):
    lx, ly, lz = extents

    def one_leaf(leaf, carry):
        x = leaf // (ly * lz)
        y = lax.rem(leaf // lz, ly)
        z = lax.rem(leaf, lz)

        def cell(p, q, r):
            return ((x + p) * (ly + 2) + y + q) * (lz + 2) + z + r

        def one_chunk(chunk, inner):
            start = pl.multiple_of(chunk * ROWS, ROWS)
            target = columns_ref[leaf, pl.ds(start, ROWS), :]
            wide = [jnp.broadcast_to(target[:, d : d + 1], (ROWS, LANES)) for d in range(3)]
            moved = [[wide[d] - float(s - 1) for s in range(3)] for d in range(3)]
            total = jnp.zeros((ROWS, LANES), jnp.float32)
            for p in range(3):
                for q in range(3):
                    for r in range(3):
                        index = cell(p, q, r)
                        gx = window_ref[index, 0:1, :] - moved[0][p]
                        gy = window_ref[index, 1:2, :] - moved[1][q]
                        gz = window_ref[index, 2:3, :] - moved[2][r]
                        squared = (gx * gx + SOFTENING * SOFTENING) + (gy * gy + gz * gz)
                        total = total + window_ref[index, 3:4, :] * lax.rsqrt(squared)
            sums_ref[leaf, pl.ds(start, ROWS), :] = total
            return inner

        lax.fori_loop(0, (counts_ref[leaf] + ROWS - 1) // ROWS, one_chunk, 0)
        return carry

    def one_row(row, carry):
        first = ((row // ly + 1) * (ly + 2) + lax.rem(row, ly) + 1) * (lz + 2) + 1
        for z in range(lz):
            columns_ref[row * lz + z] = jnp.transpose(window_ref[first + z])
        return carry

    def one_group(number, carry):
        start = pl.multiple_of(number * 8, 8)
        summed = [
            jnp.sum(jnp.transpose(sums_ref[start + k]), axis=0, keepdims=True) for k in range(8)
        ]
        out_ref[pl.ds(start, 8), :] = jnp.concatenate(summed, axis=0)
        return carry

    lax.fori_loop(0, lx * ly, one_row, 0)
    lax.fori_loop(0, lx * ly * lz, one_leaf, 0)
    lax.fori_loop(0, lx * ly * lz // 8, one_group, 0)


def near_field(window, counts, extents):
    tiles = extents[0] * extents[1] * extents[2]
    return pl.pallas_call(
        functools.partial(near_kernel, extents),
        out_shape=jax.ShapeDtypeStruct((tiles, LANES), jnp.float32),
        in_specs=[
            pl.BlockSpec(memory_space=pltpu.SMEM),
            pl.BlockSpec(memory_space=pltpu.VMEM),
        ],
        out_specs=pl.BlockSpec(memory_space=pltpu.VMEM),
        scratch_shapes=[
            pltpu.VMEM((tiles, LANES, 8), jnp.float32),
            pltpu.VMEM((tiles, LANES, LANES), jnp.float32),
        ],
        compiler_params=pltpu.CompilerParams(vmem_limit_bytes=VMEM_BYTES),
    )(counts, window)


def local_kernel(extents, leaf_ref, mid_ref, table_ref, out_ref, lined_ref, mids_ref, acc_ref):
    step = pl.program_id(0)
    dx, dy = step // 7, lax.rem(step, 7)
    lx, ly, lz = extents
    mx, my, mz = (e // 2 for e in extents)
    plane = ly * lz
    rows, small, depth = lx * plane, mx * my * mz, 7 * LANES

    def stays(length, shift, cell):
        return kept(length, shift)[cell] > 0.0

    @pl.when(step == 0)
    def _():
        acc_ref[...] = jnp.zeros_like(acc_ref)
        nothing = jnp.zeros((1, LANES), jnp.float32)

        def one_plane(x, carry):
            for t in range(7):
                for y in range(ly):
                    for z in range(lz):
                        for s in range(7):
                            lanes = slice(s * LANES, (s + 1) * LANES)
                            good = stays(ly, t, y) and stays(lz, s, z)
                            row = y * lz + z
                            value = leaf_ref[x, y + t, z + s] if good else nothing
                            lined_ref[t, x, row : row + 1, lanes] = value
            return carry

        lax.fori_loop(0, lx + 6, one_plane, 0)

        def one_shift(r, carry):
            for t in range(7):
                for x in range(mx):
                    for y in range(my):
                        for z in range(mz):
                            for s in range(7):
                                lanes = slice(s * LANES, (s + 1) * LANES)
                                good = stays(my, t, y) and stays(mz, s, z)
                                row = (x * my + y) * mz + z
                                value = mid_ref[x + r, y + t, z + s] if good else nothing
                                mids_ref[r * 7 + t, row : row + 1, lanes] = value
            return carry

        lax.fori_loop(0, 7, one_shift, 0)

    drop = jnp.where(dx == 0, 0, jnp.where(dx == 6, 1, 2))

    def masked(value, stride):
        odd = lax.rem(lax.broadcasted_iota(jnp.int32, value.shape, 0) // stride, 2)
        return jnp.where(odd == drop, 0.0, value)

    factors = [jnp.where(drop == parity, 0.0, 1.0) for parity in range(2)]
    leaf = [lined_ref[dy, dx + x] * factors[x % 2] for x in range(lx)]
    whole = jnp.concatenate(leaf + [masked(mids_ref[step], my * mz)], axis=0)
    high = whole.astype(jnp.bfloat16).astype(jnp.float32)
    both = jnp.concatenate([high, whole - high], axis=0).astype(jnp.bfloat16)
    acc_ref[...] += jnp.dot(both, table_ref[0], preferred_element_type=jnp.float32)

    @pl.when(step == 48)
    def _():
        cut = rows + small
        out_ref[...] = (
            acc_ref[:cut, :LANES] + acc_ref[:cut, LANES:] + acc_ref[cut:, :LANES]
        )


def local_expansions(leaf, mid, table, extents):
    lx, ly, lz = extents
    small = lx * ly * lz // 8
    rows, depth = lx * ly * lz + small, 7 * LANES
    return pl.pallas_call(
        functools.partial(local_kernel, extents),
        grid=(49,),
        out_shape=jax.ShapeDtypeStruct((rows, LANES), jnp.float32),
        in_specs=[
            pl.BlockSpec(memory_space=pltpu.VMEM),
            pl.BlockSpec(memory_space=pltpu.VMEM),
            pl.BlockSpec((1, depth, 2 * LANES), lambda i: (i, 0, 0)),
        ],
        out_specs=pl.BlockSpec((rows, LANES), lambda i: (0, 0)),
        scratch_shapes=[
            pltpu.VMEM((7, lx + 6, ly * lz, depth), jnp.float32),
            pltpu.VMEM((49, small, depth), jnp.float32),
            pltpu.VMEM((2 * rows, 2 * LANES), jnp.float32),
        ],
        compiler_params=pltpu.CompilerParams(vmem_limit_bytes=VMEM_BYTES),
    )(leaf, mid, table)


AXES = ("gx", "gy", "gz")


def exchange_kernel(sizes, moments_ref, packed_ref, upper_ref, window_ref, near_ref, whole_ref, send_sem, recv_sem, far_send, far_recv):
    place = [lax.axis_index(axis) for axis in AXES]
    window_ref[...] = jnp.zeros_like(window_ref)
    near_ref[...] = jnp.zeros_like(near_ref)
    lx, ly, lz = moments_ref.shape[:3]
    window_ref[3 : 3 + lx, 3 : 3 + ly, 3 : 3 + lz] = moments_ref[...]
    near_ref[1 : 1 + lx, 1 : 1 + ly, 1 : 1 + lz] = packed_ref[...]
    whole_ref[place[0], place[1], place[2]] = upper_ref[...]

    barrier = pltpu.get_barrier_semaphore()
    for d, axis in enumerate(AXES):
        for step in range(1, sizes[d]):
            peer = lax.rem(place[d] + step, sizes[d])
            pl.semaphore_signal(
                barrier, inc=1, device_id={axis: peer}, device_id_type=pl.DeviceIdType.MESH
            )
    pl.semaphore_wait(barrier, sum(sizes) - 3)

    slot = 0
    for d, axis in enumerate(AXES):
        n, me = sizes[d], place[d]
        ups, downs, shares, arrivals = [], [], [], []
        for k, (ref, width) in enumerate(((window_ref, 3), (near_ref, 1))):
            length = moments_ref.shape[d]

            def part(start):
                later = tuple(pl.ds(width, extent) for extent in moments_ref.shape[d + 1 : 3])
                return ref.at[(slice(None),) * d + (pl.ds(start, width),) + later]

            for way, (source, target) in enumerate(((length, 0), (width, length + width))):
                copy = pltpu.make_async_remote_copy(
                    src_ref=part(source),
                    dst_ref=part(target),
                    send_sem=send_sem.at[d * 4 + k * 2 + way],
                    recv_sem=recv_sem.at[d * 4 + k * 2 + way],
                    device_id={axis: me + 1 - 2 * way},
                    device_id_type=pl.DeviceIdType.MESH,
                )
                (ups, downs)[way].append(copy)

        def share(index, step, peer):
            ref = whole_ref.at[(slice(None),) * d + (index,) + tuple(place[d + 1 :])]
            return pltpu.make_async_remote_copy(
                src_ref=ref,
                dst_ref=ref,
                send_sem=far_send.at[slot + step - 1],
                recv_sem=far_recv.at[slot + step - 1],
                device_id={axis: peer},
                device_id_type=pl.DeviceIdType.MESH,
            )

        for step in range(1, n):
            peer = lax.rem(me + step, n)
            shares.append(share(me, step, peer))
            arrivals.append(share(lax.rem(me + n - step, n), step, peer))
        slot += n - 1

        @pl.when(me < n - 1)
        def _():
            for copy in ups:
                copy.start()

        @pl.when(me > 0)
        def _():
            for copy in downs:
                copy.start()

        for copy in shares:
            copy.start()

        @pl.when(me < n - 1)
        def _():
            for copy in ups:
                copy.wait_send()
            for copy in downs:
                copy.wait_recv()

        @pl.when(me > 0)
        def _():
            for copy in downs:
                copy.wait_send()
            for copy in ups:
                copy.wait_recv()

        for sent, came in zip(shares, arrivals):
            sent.wait_send()
            came.wait_recv()


def exchange(moments, packed, upper):
    sizes = tuple(lax.axis_size(axis) for axis in AXES)
    lx, ly, lz = moments.shape[:3]
    steps = sum(sizes) - 3
    full = pl.BlockSpec(memory_space=pltpu.VMEM)
    return pl.pallas_call(
        functools.partial(exchange_kernel, sizes),
        out_shape=(
            jax.ShapeDtypeStruct((lx + 6, ly + 6, lz + 6, 1, LANES), jnp.float32),
            jax.ShapeDtypeStruct((lx + 2, ly + 2, lz + 2, 8, LANES), jnp.float32),
            jax.ShapeDtypeStruct(sizes + upper.shape, jnp.float32),
        ),
        in_specs=[full] * 3,
        out_specs=(full,) * 3,
        scratch_shapes=[
            pltpu.SemaphoreType.DMA((12,)),
            pltpu.SemaphoreType.DMA((12,)),
            pltpu.SemaphoreType.DMA((steps,)),
            pltpu.SemaphoreType.DMA((steps,)),
        ],
        compiler_params=pltpu.CompilerParams(
            collective_id=0, has_side_effects=True, vmem_limit_bytes=VMEM_BYTES
        ),
    )(moments, packed, upper)


def kept(length, shift):
    cells = np.arange(length)
    return (np.abs((cells + shift - 3) // 2 - cells // 2) <= 1).astype(np.float32)


def group(moments):
    a, b, c, n = moments.shape
    paired = moments.reshape(a // 2, 2, b // 2, 2, c // 2, 2, n).transpose(0, 2, 4, 1, 3, 5, 6)
    return paired.reshape(a * b * c // 8, 8 * n)


def spread(parents, extents):
    a, b, c = extents
    apart = parents.reshape(a, b, c, 2, 2, 2, LANES).transpose(0, 3, 1, 4, 2, 5, 6)
    return apart.reshape(8 * a * b * c, LANES)


def shards(offsets, masses, counts):
    lx, ly, lz = counts.shape
    slots = masses.shape[-1]
    tiles = lx * ly * lz
    live = (jnp.arange(slots, dtype=jnp.int32)[None, None, None, :] < counts[..., None]).astype(
        jnp.float32
    )
    charge = masses * live
    flat_offsets = offsets.reshape(3, tiles, slots)
    flat_charge, flat_live = charge.reshape(tiles, slots), live.reshape(tiles, slots)

    moments0 = leaf_moments(flat_offsets, flat_charge).reshape(lx, ly, lz, LANES)
    up, down = shift_tables()
    mid = (lx // 2, ly // 2, lz // 2)
    top = (lx // 4, ly // 4, lz // 4)
    moments1 = jnp.dot(group(moments0), up, precision=HIGHEST)
    moments2 = jnp.dot(group(moments1.reshape(mid + (LANES,))), up, precision=HIGHEST)
    n_mid, n_top = moments1.shape[0], moments2.shape[0]

    upper = jnp.concatenate([moments1, moments2], axis=0)
    upper = jnp.pad(upper, ((0, -upper.shape[0] % 8), (0, 0)))
    blank = jnp.zeros_like(charge)
    packed = jnp.stack([offsets[0], offsets[1], offsets[2], charge] + [blank] * 4, axis=3)
    window0, near_window, pieces = exchange(moments0[:, :, :, None], packed, upper)
    span = pieces.shape[:3]
    place = tuple(lax.axis_index(axis) for axis in ("gx", "gy", "gz"))

    def whole_grid(part, extents):
        shaped = part.reshape(span + extents + (LANES,)).transpose(0, 3, 1, 4, 2, 5, 6)
        return shaped.reshape(tuple(span[i] * extents[i] for i in range(3)) + (LANES,))

    whole1 = whole_grid(pieces[:, :, :, :n_mid], mid)
    whole2 = whole_grid(pieces[:, :, :, n_mid : n_mid + n_top], top)

    near = near_field(near_window.reshape(-1, 8, slots), counts.reshape(-1), (lx, ly, lz))
    padded1 = jnp.pad(whole1, ((3, 3), (3, 3), (3, 3), (0, 0)))
    window1 = lax.dynamic_slice(
        padded1,
        tuple(place[i] * mid[i] for i in range(3)) + (0,),
        tuple(mid[i] + 6 for i in range(3)) + (LANES,),
    )
    locals01 = local_expansions(
        window0, window1[:, :, :, None], jnp.asarray(window_table()), (lx, ly, lz)
    )
    local0, local1 = locals01[:tiles], 0.5 * locals01[tiles:]

    grid2 = whole2.shape[:3]
    table2 = jnp.asarray(top_table(grid2))
    rows2 = []
    for a in range(top[0]):
        for b in range(top[1]):
            for c in range(top[2]):
                start = tuple(
                    grid2[i] - 1 - (place[i] * top[i] + (a, b, c)[i]) for i in range(3)
                )
                used = lax.dynamic_slice(table2, start + (0, 0), grid2 + (LANES, LANES))
                rows2.append(
                    jnp.sum(whole2[..., :, None] * used, axis=(0, 1, 2, 3))
                )
    local2 = 0.25 * jnp.stack(rows2)
    total1 = local1 + spread(jnp.dot(local2, down, precision=HIGHEST), top)
    total0 = local0 + spread(jnp.dot(total1, down, precision=HIGHEST), mid)

    outs = evaluate(flat_offsets, flat_charge, flat_live, near, total0, local0)
    return tuple(out.reshape(lx, ly, lz, slots) for out in outs)


def solution(mesh):
    placed = (P(None, "gx", "gy", "gz", None), P("gx", "gy", "gz", None), P("gx", "gy", "gz"))
    return jax.shard_map(
        shards,
        mesh=mesh,
        in_specs=placed,
        out_specs=(P("gx", "gy", "gz", None),) * 3,
        check_vma=False,
    )
```
